256 devices in a mesh: vert: 128 (over z, y, x), qcol: 2 (over core).
Axes of the slice: x: 4, y: 4, z: 8, core: 2. Of those that a mesh axis runs over, the one named last changes fastest.
Arguments:
- descriptors: bfloat16 [262144, 2048], P('vert'), may hold values from -0.8984375 to 0.8984375
- queries: bfloat16 [512, 2048], P('qcol', 'vert'), may hold values from -0.8984375 to 0.8984375
- tiles: bfloat16 [6144, 128, 128], P('vert'), may hold values from 0 to 1, as said below
- tile_cols: int32 [128, 3, 16], replicated, may hold values from 0 to 15, as said below
- part_size: int32 [128], replicated, may hold values from 1024 to 2048, as said below
Outputs:
- ranking: float32 [262144, 512], P('vert', 'qcol')
- residual: float32 [262144, 512], P('vert', 'qcol')
The draws below stay inside these ranges and needn't reach their ends.
Inputs may be any that keep to these rules, and one draw needn't show every extreme that they name: For each part d and slot j, tile_cols[d, j, :] is a permutation of 0 to 15. `part_size`: some part has exactly 2048 live vertices and some exactly 1024. tiles are sparse and nonnegative; every row and every column of B sums to at most 1.01.
All inputs are finite; a program needn't handle non-finite values.
Results may differ from the reference program's by a relative error of at most 0.0003.
Values may be sent and summed in bfloat16 or wider, within the bound.
A program may use at most 128 MiB of HBM per device.

```python
import jax
import jax.numpy as jnp
from jax import lax

DESC = 2048
TILE = 128
SLOTS = 3
ITERS = 2
VDEV = 2048
RT = 16
V = 262144
Q = 512
N_VERT = 128


def draw_tiles(key, part):
    key = jax.random.fold_in(key, 11)
    count = N_VERT * SLOTS * RT
    place_key, weight_key = jax.random.split(key)
    keys = jax.random.split(place_key, count)
    orders = jax.vmap(lambda single: jax.random.permutation(single, TILE))(keys)
    chosen = orders[:, :17]
    marks = jnp.zeros((count, TILE), jnp.float32)
    marks = jax.vmap(lambda row, picks: row.at[picks].set(1.0))(marks, chosen)
    offsets = (lax.iota(jnp.int32, TILE)[None, :] - lax.iota(jnp.int32, TILE)[:, None]) % TILE
    pattern = jnp.take(marks, offsets, axis=1)
    spread = jax.random.uniform(weight_key, (count, TILE, TILE), jnp.float32)
    weights = 1.0 - 0.8 * spread * spread * spread
    values = pattern * weights * (0.99 / (SLOTS * 17))
    return values.astype(jnp.bfloat16)


def draw_tile_cols(key, part):
    key = jax.random.fold_in(key, 12)
    keys = jax.random.split(key, N_VERT * SLOTS)
    perms = jax.vmap(lambda single: jax.random.permutation(single, RT))(keys)
    return perms.astype(jnp.int32).reshape(N_VERT, SLOTS, RT)


def draw_part_size(key, part):
    key = jax.random.fold_in(key, 13)
    first, second = jax.random.split(key)
    sizes = jax.random.randint(first, (N_VERT,), VDEV // 2, VDEV + 1).astype(jnp.int32)
    order = jax.random.permutation(second, N_VERT)
    sizes = sizes.at[order[0]].set(VDEV)
    sizes = sizes.at[order[1]].set(VDEV // 2)
    return sizes.astype(jnp.int32)


def level_of(stream_key, shape, cuts, smallest, largest):
    def one(dim, shards_of):
        heights = jax.random.uniform(jax.random.fold_in(jax.random.fold_in(stream_key, 6), dim), (shards_of,), jnp.float32, smallest / len(cuts), largest / len(cuts))
        return jnp.repeat(jnp.exp(heights), shape[dim] // shards_of).reshape((-1,) + (1,) * (len(shape) - dim - 1))

    level = one(*cuts[0])
    for cut in cuts[1:]:
        level = level * one(*cut)
    return level


def scatter_about(key, extent, scale, most, cuts=(), kind=jnp.bfloat16):
    result = jax.random.normal(key, extent, jnp.float32) * scale
    if len(cuts) > 0:
        result = level_of(key, extent, cuts, -0.22, 0.18) * result
    return jnp.clip(result, min=-most, max=most).astype(kind)


def setup_inputs(seed: int = 0) -> dict:
    key_of = jax.random.split(jax.random.key(seed), 6)
    return {
        "descriptors": scatter_about(key_of[0], (V, DESC), 0.1487, 0.8984375, ((0, 128),)),
        "queries": scatter_about(key_of[1], (Q, DESC), 0.1487, 0.8984375, ((0, 2), (1, 128))),
        "tiles": draw_tiles(jax.random.fold_in(key_of[5], 71), 0),
        "tile_cols": draw_tile_cols(jax.random.fold_in(key_of[5], 71), 0),
        "part_size": draw_part_size(jax.random.fold_in(key_of[5], 71), 0),
    }


def operate(field, blocks, tile_cols, live):
    total_q = field.shape[1]
    p3 = field.reshape(N_VERT, RT, TILE, total_q)
    forward = jnp.zeros_like(p3)
    back = jnp.zeros_like(p3)
    for slot in range(SLOTS):
        source = jnp.roll(p3, -(slot - 1), axis=0)
        picked = jnp.take_along_axis(source, tile_cols[:, slot, :, None, None], axis=1)
        forward = forward + jnp.einsum("nrab,nrbq->nraq", blocks[:, slot], picked, precision=lax.Precision.HIGHEST)
        moved = jnp.einsum("nrba,nrbq->nraq", blocks[:, slot], p3, precision=lax.Precision.HIGHEST)
        inverse = jnp.argsort(tile_cols[:, slot, :], axis=1).astype(jnp.int32)
        moved = jnp.take_along_axis(moved, inverse[:, :, None, None], axis=1)
        back = back + jnp.roll(moved, slot - 1, axis=0)
    both = (forward + back).reshape(field.shape)
    return field - 0.99 * live * (0.5 * both)


def reference(descriptors, queries, tiles, tile_cols, part_size):
    sims = jnp.dot(descriptors, queries.T, preferred_element_type=jnp.float32)
    slot_ids = jnp.arange(V, dtype=jnp.int32)
    live = ((slot_ids % VDEV) < part_size[slot_ids // VDEV]).astype(jnp.float32)[:, None]
    seeds = live * jnp.maximum(sims, 0.0) ** 3
    blocks = tiles.astype(jnp.float32).reshape(N_VERT, SLOTS, RT, TILE, TILE)
    ranking = jnp.zeros_like(seeds)
    residual = seeds
    direction = seeds
    norm_now = jnp.sum(residual * residual, axis=0)
    for step in range(ITERS):
        image = operate(direction, blocks, tile_cols, live)
        alpha = norm_now / jnp.sum(direction * image, axis=0)
        ranking = ranking + alpha[None, :] * direction
        residual = residual - alpha[None, :] * image
        norm_next = jnp.sum(residual * residual, axis=0)
        direction = residual + (norm_next / norm_now)[None, :] * direction
        norm_now = norm_next
    return ranking, residual
```

```python
import functools

import jax
import jax.numpy as jnp
from jax import lax
from jax.experimental import pallas as pl
from jax.experimental.pallas import tpu as pltpu
from jax.sharding import PartitionSpec as P

XS, YS = 4, 4
LANES = 128
STEPS = 65535.0
DAMP = 0.99
MESH = pl.DeviceIdType.MESH
F32, BF16, I32 = jnp.float32, jnp.bfloat16, jnp.int32


def kernel(
    n, desc_ref, q_ref, tiles_ref, cols_ref, size_ref,
    s0_ref, m0_ref, m1_ref, coef_ref,
    desc_v, tiles_v, nbr_tiles, w_v, qg, qcat, code_v, halo_v, scale_v, hscale_v, own_hl, halo_hl, red_v,
    cols_s, inv_s, local_sem, send_sem, recv_sem,
):
    zs = n // (XS * YS)
    rows = desc_ref.shape[0]
    rt = rows // LANES
    qdev = q_ref.shape[0]
    halves = qdev // LANES
    me = lax.axis_index("vert")
    x = lax.rem(me, XS)
    y = lax.rem(lax.div(me, XS), YS)
    z = lax.div(me, XS * YS)
    right, left = lax.rem(me + 1, n), lax.rem(me + n - 1, n)
    sizes = (XS, YS, zs)
    place = (x, y, z)

    def peer(axis, k):
        if axis == 0:
            return me - x + lax.rem(x + k, XS)
        if axis == 1:
            return me + (lax.rem(y + k, YS) - y) * XS
        return lax.rem(me + k * (XS * YS), n)

    used = [0]
    sent = []

    def send(src, dst, target):
        i = used[0]
        used[0] += 1
        copy = pltpu.make_async_remote_copy(
            src_ref=src, dst_ref=dst, send_sem=send_sem.at[i], recv_sem=recv_sem.at[i],
            device_id={"vert": target}, device_id_type=MESH,
        )
        copy.start()
        sent.append(copy)
        return copy

    partners = [peer(a, k) for a in range(3) for k in range(1, sizes[a])] + [right, left]
    barrier = pltpu.get_barrier_semaphore()
    for p in partners:
        pl.semaphore_signal(barrier, inc=1, device_id={"vert": p}, device_id_type=MESH)

    fetch_desc = pltpu.make_async_copy(desc_ref, desc_v, local_sem.at[0])
    fetch_desc.start()
    fetch_tiles = pltpu.make_async_copy(tiles_ref, tiles_v, local_sem.at[1])
    fetch_tiles.start()
    fetch_cols = []
    for i in range(3):
        part = lax.rem(me + n + i - 1, n)
        fetch_cols.append(pltpu.make_async_copy(cols_ref.at[part], cols_s.at[i], local_sem.at[2 + i]))
        fetch_cols[-1].start()

    block = q_ref.shape[1]
    eye = (lax.broadcasted_iota(I32, (block, block), 0) == lax.broadcasted_iota(I32, (block, block), 1)).astype(BF16)
    turned = lax.dot_general(eye, q_ref[...], (((1,), (1,)), ((), ())), preferred_element_type=F32).astype(BF16)
    for h in range(halves):
        qg[h, z, y, x] = turned[:, h * LANES : (h + 1) * LANES]
    live_count = size_ref[me]

    pl.semaphore_wait(barrier, len(partners))

    step1 = [send(qg.at[:, z, y, x], qg.at[:, z, y, x], peer(2, k)) for k in range(1, zs)]
    for c in step1:
        c.wait_recv()
    step2a = [send(qg.at[0, :, y, x], qg.at[0, :, y, x], peer(1, k)) for k in range(1, YS)]
    step2b = [send(qg.at[1, :, y, x], qg.at[1, :, y, x], peer(0, k)) for k in range(1, XS)]
    for c in step2a:
        c.wait_recv()
    step3a = [send(qg.at[0, :, :, x], qg.at[0, :, :, x], peer(0, k)) for k in range(1, XS)]
    for c in step2b:
        c.wait_recv()
    step3b = [send(qg.at[1, :, y], qg.at[1, :, y], peer(1, k)) for k in range(1, YS)]

    to_left = send(tiles_ref.at[pl.ds(0, rt)], nbr_tiles.at[1], left)
    to_right = send(tiles_ref.at[pl.ds(2 * rt, rt)], nbr_tiles.at[0], right)

    for c in fetch_cols:
        c.wait()
    for i in range(3):
        def invert(r, _, i=i):
            found = jnp.int32(0)
            for t in range(rt):
                found = jnp.where(cols_s[i, 2 - i, t] == r, jnp.int32(t), found)
            inv_s[i, r] = found
            return 0

        lax.fori_loop(0, rt, invert, 0)

    fetch_tiles.wait()

    def ours(r, _):
        for i in range(3):
            w_v[i, r, :, :LANES] = tiles_v[i * rt + r]
        w_v[1, r, :, LANES:] = tiles_v[rt + inv_s[1, r]].T
        return 0

    lax.fori_loop(0, rt, ours, 0)

    def gathered(h, copies):
        for c in copies:
            c.wait_recv()
        qcat[:, h * LANES : (h + 1) * LANES] = qg[h].reshape(qcat.shape[0], LANES)

    gathered(0, step3a)
    gathered(1, step3b)
    fetch_desc.wait()

    chunk = min(512, rows)

    def fold(values):
        return values.reshape(values.shape[0] // 8, 8, values.shape[1])

    def live_of(start, shape):
        return lax.broadcasted_iota(I32, shape, 0) + start < live_count

    def seed(i, carry):
        most, square = carry
        at = pl.ds(pl.multiple_of(i * chunk, chunk), chunk)
        sims = jnp.dot(desc_v[at, :], qcat[...], preferred_element_type=F32)
        pos = jnp.maximum(sims, 0.0)
        s = jnp.where(live_of(i * chunk, sims.shape), pos * pos * pos, 0.0)
        s0_ref[at, :] = s
        return jnp.maximum(most, jnp.max(fold(s), axis=0)), square + jnp.sum(fold(s * s), axis=0)

    zero = jnp.zeros((8, qdev), F32)
    most, square0 = lax.fori_loop(0, rows // chunk, seed, (zero, zero))

    def encode(it, h, src_ref, most):
        cut = slice(h * LANES, (h + 1) * LANES)
        top = jnp.max(most, axis=0, keepdims=True)
        ok = top > 1e-30
        inverse = jnp.where(ok, STEPS / jnp.where(ok, top, 1.0), 0.0)
        scale_v[it, h] = jnp.broadcast_to(top * (1.0 / STEPS), (8, LANES))

        def one(r, _):
            at = pl.ds(pl.multiple_of(r * LANES, LANES), LANES)
            v = src_ref[at, cut]
            code_v[it, h, r] = ((v * inverse + 0.5).astype(I32) - 32768).astype(jnp.int16)
            hi = v.astype(BF16)
            own_hl[h, r, :, :LANES] = hi
            own_hl[h, r, :, LANES:] = (v - hi.astype(F32)).astype(BF16)
            return 0

        lax.fori_loop(0, rt, one, 0)
        copies = []
        for side, target in ((1, left), (0, right)):
            copies.append(send(scale_v.at[it, h], hscale_v.at[it, h, side], target))
            copies.append(send(code_v.at[it, h], halo_v.at[it, h, side], target))
        return copies

    def decode(it, h, copies):
        for c in copies:
            c.wait_recv()
        for side in range(2):
            def one(r, _, side=side):
                v = halo_v[it, h, side, r].astype(I32) + 32768
                halo_hl[side, r, :, :LANES] = lax.shift_right_logical(v, 8).astype(F32).astype(BF16)
                halo_hl[side, r, :, LANES:] = lax.bitwise_and(v, 255).astype(F32).astype(BF16)
                return 0

            lax.fori_loop(0, rt, one, 0)

    def apply(it, h, out_ref, use, carry):
        cut = slice(h * LANES, (h + 1) * LANES)
        low, high = hscale_v[it, h, 0][:1], hscale_v[it, h, 1][:1]

        def one(r, carry):
            at = pl.ds(pl.multiple_of(r * LANES, LANES), LANES)
            from_left = jnp.dot(
                w_v[0, r],
                jnp.concatenate([halo_hl[0, cols_s[1, 0, r]], halo_hl[0, inv_s[0, r]]], axis=0),
                preferred_element_type=F32,
            )
            from_own = jnp.dot(
                w_v[1, r],
                jnp.concatenate([own_hl[h, cols_s[1, 1, r]], own_hl[h, inv_s[1, r]]], axis=0),
                preferred_element_type=F32,
            )
            from_right = jnp.dot(
                w_v[2, r],
                jnp.concatenate([halo_hl[1, cols_s[1, 2, r]], halo_hl[1, inv_s[2, r]]], axis=0),
                preferred_element_type=F32,
            )
            total = (from_left[:, :LANES] * 256.0 + from_left[:, LANES:]) * low
            total = total + (from_own[:, :LANES] + from_own[:, LANES:])
            total = total + (from_right[:, :LANES] * 256.0 + from_right[:, LANES:]) * high
            m = jnp.where(live_of(r * LANES, total.shape), 0.5 * total, 0.0)
            out_ref[at, cut] = m
            return use(carry, at, cut, m)

        return lax.fori_loop(0, rt, one, carry)

    def total_of(p, first, second):
        row = lax.broadcasted_iota(I32, (8, qdev), 0)
        value = jnp.where(
            row == 0,
            jnp.sum(first, axis=0, keepdims=True),
            jnp.where(row == 1, jnp.sum(second, axis=0, keepdims=True), 0.0),
        )
        base = 0
        for axis in range(3):
            mine = base + place[axis]
            red_v[p, mine] = value
            copies = [send(red_v.at[p, mine], red_v.at[p, mine], peer(axis, k)) for k in range(1, sizes[axis])]
            for c in copies:
                c.wait_recv()
            value = red_v[p, base]
            for k in range(1, sizes[axis]):
                value = value + red_v[p, base + k]
            base += sizes[axis]
        return value[0:1], value[1:2]

    halo0 = [encode(0, h, s0_ref, most[:, h * LANES : (h + 1) * LANES]) for h in range(halves)]

    for side, copy in ((1, to_left), (0, to_right)):
        copy.wait_recv()

    def theirs(r, _):
        w_v[0, r, :, LANES:] = nbr_tiles[0, inv_s[0, r]].T
        w_v[2, r, :, LANES:] = nbr_tiles[1, inv_s[2, r]].T
        return 0

    lax.fori_loop(0, rt, theirs, 0)

    def first_use(carry, at, cut, m):
        most, curve = carry
        s0 = s0_ref[at, cut]
        return jnp.maximum(most, jnp.max(fold(m), axis=0)), curve + jnp.sum(fold(s0 * (s0 - DAMP * m)), axis=0)

    small = jnp.zeros((8, LANES), F32)
    halo1, curves = [], []
    for h in range(halves):
        decode(0, h, halo0[h])
        most, curve = apply(0, h, m0_ref, first_use, (small, small))
        curves.append(curve)
        halo1.append(encode(1, h, m0_ref, most))

    rr0, curve0 = total_of(0, square0, jnp.concatenate(curves, axis=1))
    alpha0 = rr0 / curve0

    def residual_square(r, square):
        at = pl.ds(pl.multiple_of(r * LANES, LANES), LANES)
        s0 = s0_ref[at, :]
        r1 = s0 - alpha0 * (s0 - DAMP * m0_ref[at, :])
        return square + jnp.sum(fold(r1 * r1), axis=0)

    square1 = lax.fori_loop(0, rt, residual_square, zero)
    rr1, _ = total_of(1, square1, square1)
    beta = rr1 / rr0

    def second_use(curve, at, cut, m1):
        s0, m0 = s0_ref[at, cut], m0_ref[at, cut]
        a, b = alpha0[:, cut], beta[:, cut]
        d1 = (s0 - a * (s0 - DAMP * m0)) + b * s0
        image = d1 - DAMP * ((1.0 + b) * m0 - a * (m0 - DAMP * m1))
        return curve + jnp.sum(fold(d1 * image), axis=0)

    curves = []
    for h in range(halves):
        decode(1, h, halo1[h])
        curves.append(apply(1, h, m1_ref, second_use, small))
    curve = jnp.concatenate(curves, axis=1)
    curve1, _ = total_of(2, curve, curve)
    alpha1 = rr1 / curve1
    row = lax.broadcasted_iota(I32, (8, qdev), 0)
    coef_ref[...] = jnp.where(row == 0, alpha0, jnp.where(row == 1, beta, alpha1))

    for c in sent:
        c.wait_send()


def body(descriptors, queries, tiles, tile_cols, part_size):
    n = lax.axis_size("vert")
    rows, width = descriptors.shape
    qdev, block = queries.shape
    rt = rows // LANES
    halves = qdev // LANES
    zs = n // (XS * YS)
    field = pltpu.VMEM((rows, qdev), F32)
    hops = XS + YS + zs - 3
    copies = (zs - 1 + 2 * (XS + YS - 2)) + 2 + 2 * halves * 4 + 3 * hops
    s0, m0, m1, coef = pl.pallas_call(
        functools.partial(kernel, n),
        out_shape=(field, field, field, pltpu.VMEM((8, qdev), F32)),
        in_specs=[
            pl.BlockSpec(memory_space=pl.ANY),
            pl.BlockSpec(memory_space=pltpu.VMEM),
            pl.BlockSpec(memory_space=pl.ANY),
            pl.BlockSpec(memory_space=pl.ANY),
            pl.BlockSpec(memory_space=pltpu.SMEM),
        ],
        out_specs=[pl.BlockSpec(memory_space=pltpu.VMEM)] * 4,
        scratch_shapes=[
            pltpu.VMEM((rows, width), BF16),
            pltpu.VMEM((3 * rt, LANES, LANES), BF16),
            pltpu.VMEM((2, rt, LANES, LANES), BF16),
            pltpu.VMEM((3, rt, LANES, 2 * LANES), BF16),
            pltpu.VMEM((halves, zs, YS, XS, block, LANES), BF16),
            pltpu.VMEM((width, qdev), BF16),
            pltpu.VMEM((2, halves, rt, LANES, LANES), jnp.int16),
            pltpu.VMEM((2, halves, 2, rt, LANES, LANES), jnp.int16),
            pltpu.VMEM((2, halves, 8, LANES), F32),
            pltpu.VMEM((2, halves, 2, 8, LANES), F32),
            pltpu.VMEM((halves, rt, LANES, 2 * LANES), BF16),
            pltpu.VMEM((2, rt, LANES, 2 * LANES), BF16),
            pltpu.VMEM((3, XS + YS + zs, 8, qdev), F32),
            pltpu.SMEM((3, 3, rt), I32),
            pltpu.SMEM((3, rt), I32),
            pltpu.SemaphoreType.DMA((5,)),
            pltpu.SemaphoreType.DMA((copies,)),
            pltpu.SemaphoreType.DMA((copies,)),
        ],
        compiler_params=pltpu.CompilerParams(
            collective_id=0, has_side_effects=True, vmem_limit_bytes=40 * 2**20
        ),
    )(descriptors, queries, tiles, tile_cols, part_size)
    alpha0, beta, alpha1 = coef[0:1], coef[1:2], coef[2:3]
    r1 = s0 - alpha0 * (s0 - DAMP * m0)
    d1 = r1 + beta * s0
    image = d1 - DAMP * ((1.0 + beta) * m0 - alpha0 * (m0 - DAMP * m1))
    return alpha0 * s0 + alpha1 * d1, r1 - alpha1 * image


def solution(mesh):
    placed = (P("vert", None), P("qcol", "vert"), P("vert", None, None), P(), P())
    return jax.shard_map(
        body,
        mesh=mesh,
        in_specs=placed,
        out_specs=(P("vert", "qcol"), P("vert", "qcol")),
        check_vma=False,
    )
```

```python
import functools

import jax
import jax.numpy as jnp
from jax import lax
from jax.experimental import pallas as pl
from jax.experimental.pallas import tpu as pltpu
from jax.sharding import PartitionSpec as P

XS, YS = 4, 4
LANES = 128
STEPS = 65535.0
DAMP = 0.99
MESH = pl.DeviceIdType.MESH
F32, BF16, I32 = jnp.float32, jnp.bfloat16, jnp.int32


def kernel(
    n, desc_ref, q_ref, tiles_ref, cols_ref, size_ref,
    s0_ref, m0_ref, m1_ref, coef_ref,
    desc_v, tiles_v, nbr_tiles, w_v, qg, qcat, code_v, halo_v, scale_v, hscale_v, own_hl, halo_hl, red_v,
    cols_s, size_s, inv_s, local_sem, send_sem, recv_sem,
):
    zs = n // (XS * YS)
    rows = desc_ref.shape[0]
    rt = rows // LANES
    qdev = q_ref.shape[1]
    halves = qdev // LANES
    me = lax.axis_index("vert")
    x = lax.rem(me, XS)
    y = lax.rem(lax.div(me, XS), YS)
    z = lax.div(me, XS * YS)
    right, left = lax.rem(me + 1, n), lax.rem(me + n - 1, n)
    sizes = (XS, YS, zs)
    core, cores = lax.axis_index("qcol"), lax.axis_size("qcol")
    plane = XS * YS
    spot = lax.rem(me, plane)

    def peer(axis, k):
        if axis == 0:
            return me - x + lax.rem(x + k, XS)
        if axis == 1:
            return me + (lax.rem(y + k, YS) - y) * XS
        return lax.rem(me + k * (XS * YS), n)

    used = [0]
    sent = []

    def send(src, dst, target):
        i = used[0]
        used[0] += 1
        copy = pltpu.make_async_remote_copy(
            src_ref=src, dst_ref=dst, send_sem=send_sem.at[i], recv_sem=recv_sem.at[i],
            device_id=target if isinstance(target, dict) else {"vert": target}, device_id_type=MESH,
        )
        copy.start()
        sent.append(copy)
        return copy

    in_plane = [me - spot + lax.rem(y + j, YS) * XS + lax.rem(x + i, XS) for j in range(YS) for i in range(XS) if i or j]
    along_z = [peer(2, k) for k in range(1, zs)]
    others = [{"qcol": lax.rem(core + k, cores)} for k in range(1, cores)]
    partners = [{"vert": p} for p in in_plane + along_z + [right, left]] + others
    barrier = pltpu.get_barrier_semaphore()
    for p in partners:
        pl.semaphore_signal(barrier, inc=1, device_id=p, device_id_type=MESH)

    fetch_desc = pltpu.make_async_copy(desc_ref, desc_v, local_sem.at[0])
    fetch_desc.start()
    fetch_tiles = pltpu.make_async_copy(tiles_ref, tiles_v, local_sem.at[1])
    fetch_tiles.start()
    fetch_cols = pltpu.make_async_copy(cols_ref, cols_s, local_sem.at[2])
    fetch_cols.start()
    fetch_size = pltpu.make_async_copy(size_ref, size_s, local_sem.at[3])
    fetch_size.start()
    fetch_q = [
        pltpu.make_async_copy(q_ref.at[:, h * LANES : (h + 1) * LANES], qg.at[h, z, y, x], local_sem.at[4 + h])
        for h in range(halves)
    ]
    for c in fetch_q:
        c.start()

    fetch_cols.wait()
    fetch_size.wait()
    live_count = size_s[me]
    parts = (left, me, right)
    for i in range(3):
        def invert(r, _, i=i):
            found = jnp.int32(0)
            for t in range(rt):
                found = jnp.where(cols_s[2 - i, t, parts[i]] == r, jnp.int32(t), found)
            inv_s[i, r] = found
            return 0

        lax.fori_loop(0, rt, invert, 0)

    fetch_tiles.wait()

    def ours(r, _):
        for i in range(3):
            w_v[i, r, :, :LANES] = tiles_v[i * rt + r]
        w_v[1, r, :, LANES:] = tiles_v[rt + inv_s[1, r]].T
        return 0

    lax.fori_loop(0, rt, ours, 0)

    for c in fetch_q:
        c.wait()
    pl.semaphore_wait(barrier, len(partners))

    step1 = [send(qg.at[:, z, y, x], qg.at[:, z, y, x], peer(2, k)) for k in range(1, zs)]
    for c in step1:
        c.wait_recv()
    step2a = [send(qg.at[0, :, y, x], qg.at[0, :, y, x], peer(1, k)) for k in range(1, YS)]
    step2b = [send(qg.at[1, :, y, x], qg.at[1, :, y, x], peer(0, k)) for k in range(1, XS)]
    for c in step2a:
        c.wait_recv()
    step3a = [send(qg.at[0, :, :, x], qg.at[0, :, :, x], peer(0, k)) for k in range(1, XS)]
    for c in step2b:
        c.wait_recv()
    step3b = [send(qg.at[1, :, y], qg.at[1, :, y], peer(1, k)) for k in range(1, YS)]

    def gathered(h, copies):
        for c in copies:
            c.wait_recv()
        qcat[:, h * LANES : (h + 1) * LANES] = qg[h].reshape(qcat.shape[0], LANES)

    gathered(0, step3a)
    gathered(1, step3b)

    share = rt // cores
    part = pl.ds(core * share, share)
    swapped = [
        send(tiles_v.at[pl.ds(core * share, share)], nbr_tiles.at[1, part], left),
        send(tiles_v.at[pl.ds(2 * rt + core * share, share)], nbr_tiles.at[0, part], right),
    ]
    fetch_desc.wait()

    chunk = min(512, rows)

    def fold(values):
        return values.reshape(values.shape[0] // 8, 8, values.shape[1])

    def live_of(start, shape):
        return lax.broadcasted_iota(I32, shape, 0) + start < live_count

    def seed(i, carry):
        most, square = carry
        at = pl.ds(pl.multiple_of(i * chunk, chunk), chunk)
        sims = jnp.dot(desc_v[at, :], qcat[...], preferred_element_type=F32)
        pos = jnp.maximum(sims, 0.0)
        s = jnp.where(live_of(i * chunk, sims.shape), pos * pos * pos, 0.0)
        s0_ref[at, :] = s
        return jnp.maximum(most, jnp.max(fold(s), axis=0)), square + jnp.sum(fold(s * s), axis=0)

    zero = jnp.zeros((8, qdev), F32)
    most, square0 = lax.fori_loop(0, rows // chunk, seed, (zero, zero))

    def encode(it, h, src_ref, most):
        cut = slice(h * LANES, (h + 1) * LANES)
        top = jnp.max(most, axis=0, keepdims=True)
        ok = top > 1e-30
        inverse = jnp.where(ok, STEPS / jnp.where(ok, top, 1.0), 0.0)
        scale_v[it, h] = jnp.broadcast_to(top * (1.0 / STEPS), (8, LANES))

        def one(r, _):
            at = pl.ds(pl.multiple_of(r * LANES, LANES), LANES)
            v = src_ref[at, cut]
            code_v[it, h, r] = ((v * inverse + 0.5).astype(I32) - 32768).astype(jnp.int16)
            hi = v.astype(BF16)
            own_hl[h, r, :, :LANES] = hi
            own_hl[h, r, :, LANES:] = (v - hi.astype(F32)).astype(BF16)
            return 0

        lax.fori_loop(0, rt, one, 0)
        copies = []
        for side, target in ((1, left), (0, right)):
            copies.append(send(scale_v.at[it, h], hscale_v.at[it, h, side], target))
            copies.append(send(code_v.at[it, h], halo_v.at[it, h, side], target))
        return copies

    def decode(it, h, copies):
        for c in copies:
            c.wait_recv()
        for side in range(2):
            def one(r, _, side=side):
                v = halo_v[it, h, side, r].astype(I32) + 32768
                halo_hl[side, r, :, :LANES] = lax.shift_right_logical(v, 8).astype(F32).astype(BF16)
                halo_hl[side, r, :, LANES:] = lax.bitwise_and(v, 255).astype(F32).astype(BF16)
                return 0

            lax.fori_loop(0, rt, one, 0)

    def apply(it, h, out_ref, use, carry):
        cut = slice(h * LANES, (h + 1) * LANES)
        low, high = hscale_v[it, h, 0][:1], hscale_v[it, h, 1][:1]

        def one(r, carry):
            at = pl.ds(pl.multiple_of(r * LANES, LANES), LANES)
            from_left = jnp.dot(
                w_v[0, r],
                jnp.concatenate([halo_hl[0, cols_s[0, r, me]], halo_hl[0, inv_s[0, r]]], axis=0),
                preferred_element_type=F32,
            )
            from_own = jnp.dot(
                w_v[1, r],
                jnp.concatenate([own_hl[h, cols_s[1, r, me]], own_hl[h, inv_s[1, r]]], axis=0),
                preferred_element_type=F32,
            )
            from_right = jnp.dot(
                w_v[2, r],
                jnp.concatenate([halo_hl[1, cols_s[2, r, me]], halo_hl[1, inv_s[2, r]]], axis=0),
                preferred_element_type=F32,
            )
            total = (from_left[:, :LANES] * 256.0 + from_left[:, LANES:]) * low
            total = total + (from_own[:, :LANES] + from_own[:, LANES:])
            total = total + (from_right[:, :LANES] * 256.0 + from_right[:, LANES:]) * high
            m = jnp.where(live_of(r * LANES, total.shape), 0.5 * total, 0.0)
            out_ref[at, cut] = m
            return use(carry, at, cut, m)

        return lax.fori_loop(0, rt, one, carry)

    def sum_start(p, partials):
        row = lax.broadcasted_iota(I32, (8, qdev), 0)
        value = jnp.zeros((8, qdev), F32)
        for i, partial in enumerate(partials):
            value = jnp.where(row == i, jnp.sum(partial, axis=0, keepdims=True), value)
        red_v[p, spot] = value
        return [send(red_v.at[p, spot], red_v.at[p, spot], t) for t in in_plane]

    def added(p, first, count):
        value = red_v[p, first]
        for k in range(1, count):
            value = value + red_v[p, first + k]
        return value

    def sum_middle(p, copies):
        for c in copies:
            c.wait_recv()
        mine = plane + z
        red_v[p, mine] = added(p, 0, plane)
        return [send(red_v.at[p, mine], red_v.at[p, mine], t) for t in along_z]

    def sum_end(p, copies):
        for c in copies:
            c.wait_recv()
        return added(p, plane, zs)

    halo0 = [encode(0, h, s0_ref, most[:, h * LANES : (h + 1) * LANES]) for h in range(halves)]

    passed = []
    for side, copy in ((1, swapped[0]), (0, swapped[1])):
        copy.wait_recv()
        for other in others:
            passed.append(send(nbr_tiles.at[side, part], nbr_tiles.at[side, part], other))
    for c in passed:
        c.wait_recv()

    def theirs(r, _):
        w_v[0, r, :, LANES:] = nbr_tiles[0, inv_s[0, r]].T
        w_v[2, r, :, LANES:] = nbr_tiles[1, inv_s[2, r]].T
        return 0

    lax.fori_loop(0, rt, theirs, 0)

    def first_use(carry, at, cut, m):
        most, curve = carry
        s0 = s0_ref[at, cut]
        return jnp.maximum(most, jnp.max(fold(m), axis=0)), curve + jnp.sum(fold(s0 * (s0 - DAMP * m)), axis=0)

    small = jnp.zeros((8, LANES), F32)
    halo1, curves = [], []
    for h in range(halves):
        decode(0, h, halo0[h])
        most, curve = apply(0, h, m0_ref, first_use, (small, small))
        curves.append(curve)
        halo1.append(encode(1, h, m0_ref, most))

    on_way = sum_start(0, [square0, jnp.concatenate(curves, axis=1)])
    decode(1, 0, halo1[0])
    on_way = sum_middle(0, on_way)
    for h in range(halves - 1):
        if h:
            decode(1, h, halo1[h])
        apply(1, h, m1_ref, lambda carry, at, cut, m: carry, 0)
    total = sum_end(0, on_way)
    rr0, curve0 = total[0:1], total[1:2]
    alpha0 = rr0 / curve0

    def second_use(carry, at, cut, m1):
        s0, m0, a = s0_ref[at, cut], m0_ref[at, cut], alpha0[:, cut]
        s1 = s0 - DAMP * m0
        r1 = s0 - a * s1
        image = r1 - DAMP * (m0 - a * (m0 - DAMP * m1))
        return tuple(c + jnp.sum(fold(r1 * v), axis=0) for c, v in zip(carry, (r1, image, s1), strict=True))

    def second_pass(h):
        cut = slice(h * LANES, (h + 1) * LANES)

        def one(r, carry):
            at = pl.ds(pl.multiple_of(r * LANES, LANES), LANES)
            return second_use(carry, at, cut, m1_ref[at, cut])

        return lax.fori_loop(0, rt, one, (small, small, small))

    dots = [second_pass(h) for h in range(halves - 1)]
    decode(1, halves - 1, halo1[halves - 1])
    dots.append(apply(1, halves - 1, m1_ref, second_use, (small, small, small)))
    total = sum_end(1, sum_middle(1, sum_start(1, [jnp.concatenate(d, axis=1) for d in zip(*dots, strict=True)])))
    rr1 = total[0:1]
    beta = rr1 / rr0
    curve1 = total[1:2] + beta * (2.0 * total[2:3] + beta * curve0)
    alpha1 = rr1 / curve1
    row = lax.broadcasted_iota(I32, (8, qdev), 0)
    coef_ref[...] = jnp.where(row == 0, alpha0, jnp.where(row == 1, beta, alpha1))

    for c in sent:
        c.wait_send()


def body(descriptors, queries, tiles, tile_cols, part_size):
    n = lax.axis_size("vert")
    rows, width = descriptors.shape
    qdev, block = queries.shape
    rt = rows // LANES
    halves = qdev // LANES
    zs = n // (XS * YS)
    field = pltpu.VMEM((rows, qdev), F32)
    cores = lax.axis_size("qcol")
    copies = (zs - 1 + 2 * (XS + YS - 2)) + 2 * cores + 2 * halves * 4 + 2 * (XS * YS + zs - 2)
    s0, m0, m1, coef = pl.pallas_call(
        functools.partial(kernel, n),
        out_shape=(field, field, field, pltpu.VMEM((8, qdev), F32)),
        in_specs=[pl.BlockSpec(memory_space=pltpu.HBM)] * 5,
        out_specs=[pl.BlockSpec(memory_space=pltpu.VMEM)] * 4,
        scratch_shapes=[
            pltpu.VMEM((rows, width), BF16),
            pltpu.VMEM((3 * rt, LANES, LANES), BF16),
            pltpu.VMEM((2, rt, LANES, LANES), BF16),
            pltpu.VMEM((3, rt, LANES, 2 * LANES), BF16),
            pltpu.VMEM((halves, zs, YS, XS, block, LANES), BF16),
            pltpu.VMEM((width, qdev), BF16),
            pltpu.VMEM((2, halves, rt, LANES, LANES), jnp.int16),
            pltpu.VMEM((2, halves, 2, rt, LANES, LANES), jnp.int16),
            pltpu.VMEM((2, halves, 8, LANES), F32),
            pltpu.VMEM((2, halves, 2, 8, LANES), F32),
            pltpu.VMEM((halves, rt, LANES, 2 * LANES), BF16),
            pltpu.VMEM((2, rt, LANES, 2 * LANES), BF16),
            pltpu.VMEM((2, XS * YS + zs, 8, qdev), F32),
            pltpu.SMEM((3, rt, n), I32),
            pltpu.SMEM((n,), I32),
            pltpu.SMEM((3, rt), I32),
            pltpu.SemaphoreType.DMA((4 + halves,)),
            pltpu.SemaphoreType.DMA((copies,)),
            pltpu.SemaphoreType.DMA((copies,)),
        ],
        compiler_params=pltpu.CompilerParams(
            collective_id=0, has_side_effects=True, vmem_limit_bytes=40 * 2**20
        ),
    )(*(pltpu.with_memory_space_constraint(v, pltpu.HBM) for v in (descriptors, queries.T, tiles, jnp.transpose(tile_cols, (1, 2, 0)), part_size)))
    alpha0, beta, alpha1 = coef[0:1], coef[1:2], coef[2:3]
    r1 = s0 - alpha0 * (s0 - DAMP * m0)
    d1 = r1 + beta * s0
    image = d1 - DAMP * ((1.0 + beta) * m0 - alpha0 * (m0 - DAMP * m1))
    return alpha0 * s0 + alpha1 * d1, r1 - alpha1 * image


def solution(mesh):
    placed = (P("vert", None), P("qcol", "vert"), P("vert", None, None), P(), P())
    return jax.shard_map(
        body,
        mesh=mesh,
        in_specs=placed,
        out_specs=(P("vert", "qcol"), P("vert", "qcol")),
        check_vma=False,
    )
```

```python
import functools

import jax
import jax.numpy as jnp
from jax import lax
from jax.experimental import pallas as pl
from jax.experimental.pallas import tpu as pltpu
from jax.sharding import PartitionSpec as P

XS, YS = 4, 4
LANES = 128
STEPS = 65535.0
DAMP = 0.99
PIECES = 8
MESH = pl.DeviceIdType.MESH
F32, BF16, I32 = jnp.float32, jnp.bfloat16, jnp.int32


def kernel(
    n, desc_ref, q_ref, tiles_ref, cols_ref, size_ref,
    s0_ref, m0_ref, m1_ref, coef_ref,
    desc_v, tiles_v, nbr_tiles, w_v, qg, qcat, code_v, halo_v, scale_v, hscale_v, own_hl, halo_hl, red_v,
    cols_s, size_s, inv_s, local_sem, send_sem, recv_sem,
):
    zs = n // (XS * YS)
    rows = desc_ref.shape[0]
    rt = rows // LANES
    qdev = q_ref.shape[1]
    halves = qdev // LANES
    me = lax.axis_index("vert")
    x = lax.rem(me, XS)
    y = lax.rem(lax.div(me, XS), YS)
    z = lax.div(me, XS * YS)
    right, left = lax.rem(me + 1, n), lax.rem(me + n - 1, n)
    sizes = (XS, YS, zs)
    core, cores = lax.axis_index("qcol"), lax.axis_size("qcol")
    plane = XS * YS
    spot = lax.rem(me, plane)

    def peer(axis, k):
        if axis == 0:
            return me - x + lax.rem(x + k, XS)
        if axis == 1:
            return me + (lax.rem(y + k, YS) - y) * XS
        return lax.rem(me + k * (XS * YS), n)

    used = [0]
    sent = []

    def send(src, dst, target):
        i = used[0]
        used[0] += 1
        copy = pltpu.make_async_remote_copy(
            src_ref=src, dst_ref=dst, send_sem=send_sem.at[i], recv_sem=recv_sem.at[i],
            device_id=target if isinstance(target, dict) else {"vert": target}, device_id_type=MESH,
        )
        copy.start()
        sent.append(copy)
        return copy

    in_plane = [me - spot + lax.rem(y + j, YS) * XS + lax.rem(x + i, XS) for j in range(YS) for i in range(XS) if i or j]
    along_z = [peer(2, k) for k in range(1, zs)]
    others = [{"qcol": lax.rem(core + k, cores)} for k in range(1, cores)]
    partners = [{"vert": p} for p in in_plane + along_z + [right, left]] + others
    barrier = pltpu.get_barrier_semaphore()
    for p in partners:
        pl.semaphore_signal(barrier, inc=1, device_id=p, device_id_type=MESH)

    fetch_desc = pltpu.make_async_copy(desc_ref, desc_v, local_sem.at[0])
    fetch_desc.start()
    fetch_tiles = pltpu.make_async_copy(tiles_ref, tiles_v, local_sem.at[1])
    fetch_tiles.start()
    fetch_cols = pltpu.make_async_copy(cols_ref, cols_s, local_sem.at[2])
    fetch_cols.start()
    fetch_size = pltpu.make_async_copy(size_ref, size_s, local_sem.at[3])
    fetch_size.start()
    fetch_q = [
        pltpu.make_async_copy(q_ref.at[:, h * LANES : (h + 1) * LANES], qg.at[(h, *at, z)], local_sem.at[4 + h])
        for h, at in ((0, (x, y)), (1, (y, x)))
    ]
    for c in fetch_q:
        c.start()

    fetch_cols.wait()
    fetch_size.wait()
    live_count = size_s[me]
    parts = (left, me, right)
    for i in range(3):
        def invert(r, _, i=i):
            found = jnp.int32(0)
            for t in range(rt):
                found = jnp.where(cols_s[2 - i, t, parts[i]] == r, jnp.int32(t), found)
            inv_s[i, r] = found
            return 0

        lax.fori_loop(0, rt, invert, 0)

    fetch_tiles.wait()

    def ours(r, _):
        for i in range(3):
            w_v[i, r, :, :LANES] = tiles_v[i * rt + r]
        w_v[1, r, :, LANES:] = tiles_v[rt + inv_s[1, r]].T
        return 0

    lax.fori_loop(0, rt, ours, 0)

    for c in fetch_q:
        c.wait()
    pl.semaphore_wait(barrier, len(partners))

    step1 = [[send(qg.at[(h, *at, z)], qg.at[(h, *at, z)], t) for t in along_z] for h, at in ((0, (x, y)), (1, (y, x)))]
    for c in step1[0]:
        c.wait_recv()
    step2a = [send(qg.at[0, x, y], qg.at[0, x, y], peer(1, k)) for k in range(1, YS)]
    for c in step1[1]:
        c.wait_recv()
    step2b = [send(qg.at[1, y, x], qg.at[1, y, x], peer(0, k)) for k in range(1, XS)]
    for c in step2a:
        c.wait_recv()
    step3a = [send(qg.at[0, x], qg.at[0, x], peer(0, k)) for k in range(1, XS)]
    for c in step2b:
        c.wait_recv()
    step3b = [send(qg.at[1, y], qg.at[1, y], peer(1, k)) for k in range(1, YS)]

    def gathered(h, copies):
        for c in copies:
            c.wait_recv()
        block = qg.shape[4]
        for zz in range(zs):
            for yy in range(YS):
                for xx in range(XS):
                    at = ((zz * YS + yy) * XS + xx) * block
                    qcat[at : at + block, h * LANES : (h + 1) * LANES] = qg[(h, *((xx, yy) if h == 0 else (yy, xx)), zz)]

    gathered(0, step3a)
    share = rt // cores
    part = pl.ds(core * share, share)
    swapped = [
        send(tiles_v.at[pl.ds(core * share, share)], nbr_tiles.at[1, part], left),
        send(tiles_v.at[pl.ds(2 * rt + core * share, share)], nbr_tiles.at[0, part], right),
    ]
    gathered(1, step3b)

    fetch_desc.wait()

    chunk = min(512, rows)

    def fold(values):
        return values.reshape(values.shape[0] // 8, 8, values.shape[1])

    def live_of(start, shape):
        return lax.broadcasted_iota(I32, shape, 0) + start < live_count

    def seed(i, carry):
        most, square = carry
        at = pl.ds(pl.multiple_of(i * chunk, chunk), chunk)
        sims = jnp.dot(desc_v[at, :], qcat[...], preferred_element_type=F32)
        pos = jnp.maximum(sims, 0.0)
        s = jnp.where(live_of(i * chunk, sims.shape), pos * pos * pos, 0.0)
        s0_ref[at, :] = s
        return jnp.maximum(most, jnp.max(fold(s), axis=0)), square + jnp.sum(fold(s * s), axis=0)

    zero = jnp.zeros((8, qdev), F32)
    most, square0 = lax.fori_loop(0, rows // chunk, seed, (zero, zero))

    def encode(it, h, src_ref, most):
        cut = slice(h * LANES, (h + 1) * LANES)
        top = jnp.max(most, axis=0, keepdims=True)
        ok = top > 1e-30
        inverse = jnp.where(ok, STEPS / jnp.where(ok, top, 1.0), 0.0)
        scale_v[it, h] = jnp.broadcast_to(top * (1.0 / STEPS), (8, LANES))

        def one(r, _):
            at = pl.ds(pl.multiple_of(r * LANES, LANES), LANES)
            v = src_ref[at, cut]
            code_v[it, h, r] = ((v * inverse + 0.5).astype(I32) - 32768).astype(jnp.int16)
            hi = v.astype(BF16)
            own_hl[h, r, :, :LANES] = hi
            own_hl[h, r, :, LANES:] = (v - hi.astype(F32)).astype(BF16)
            return 0

        lax.fori_loop(0, rt, one, 0)

    def both_ways(it, h, after=()):
        for c in after:
            c.wait_send()
            sent[:] = [s for s in sent if s is not c]
        copies = []
        for side, target in ((1, left), (0, right)):
            copies.append(send(scale_v.at[it, h], hscale_v.at[it, h, side], target))
            copies.append(send(code_v.at[it, h], halo_v.at[it, h, side], target))
        return copies

    def decode(it, h, copies):
        for c in copies:
            c.wait_recv()
        for side in range(2):
            def one(r, _, side=side):
                v = halo_v[it, h, side, r].astype(I32) + 32768
                halo_hl[side, r, :, :LANES] = lax.shift_right_logical(v, 8).astype(F32).astype(BF16)
                halo_hl[side, r, :, LANES:] = lax.bitwise_and(v, 255).astype(F32).astype(BF16)
                return 0

            lax.fori_loop(0, rt, one, 0)

    def apply_own(h, out_ref):
        cut = slice(h * LANES, (h + 1) * LANES)

        def one(r, _):
            at = pl.ds(pl.multiple_of(r * LANES, LANES), LANES)
            from_own = jnp.dot(
                w_v[1, r],
                jnp.concatenate([own_hl[h, cols_s[1, r, me]], own_hl[h, inv_s[1, r]]], axis=0),
                preferred_element_type=F32,
            )
            out_ref[at, cut] = from_own[:, :LANES] + from_own[:, LANES:]
            return 0

        lax.fori_loop(0, rt, one, 0, unroll=4)

    def apply(it, h, out_ref, use, carry):
        cut = slice(h * LANES, (h + 1) * LANES)
        low, high = hscale_v[it, h, 0][:1], hscale_v[it, h, 1][:1]

        def one(r, carry):
            at = pl.ds(pl.multiple_of(r * LANES, LANES), LANES)
            from_left = jnp.dot(
                w_v[0, r],
                jnp.concatenate([halo_hl[0, cols_s[0, r, me]], halo_hl[0, inv_s[0, r]]], axis=0),
                preferred_element_type=F32,
            )
            from_right = jnp.dot(
                w_v[2, r],
                jnp.concatenate([halo_hl[1, cols_s[2, r, me]], halo_hl[1, inv_s[2, r]]], axis=0),
                preferred_element_type=F32,
            )
            total = (from_left[:, :LANES] * 256.0 + from_left[:, LANES:]) * low
            total = total + out_ref[at, cut]
            total = total + (from_right[:, :LANES] * 256.0 + from_right[:, LANES:]) * high
            m = jnp.where(live_of(r * LANES, total.shape), 0.5 * total, 0.0)
            out_ref[at, cut] = m
            return use(carry, at, cut, m)

        return lax.fori_loop(0, rt, one, carry, unroll=4)

    def sum_start(p, partials):
        row = lax.broadcasted_iota(I32, (8, LANES), 0)
        value = jnp.zeros((8, LANES), F32)
        for i, partial in enumerate(partials):
            for h in range(halves):
                sums = jnp.sum(partial[:, h * LANES : (h + 1) * LANES], axis=0, keepdims=True)
                value = jnp.where(row == i * halves + h, sums, value)
        red_v[p, z] = value
        return [send(red_v.at[p, z], red_v.at[p, z], t) for t in along_z]

    def added(p, first, count):
        value = red_v[p, first]
        for k in range(1, count):
            value = value + red_v[p, first + k]
        return value

    def sum_middle(p, copies):
        for c in copies:
            c.wait_recv()
        mine = zs + spot
        red_v[p, mine] = added(p, 0, zs)
        return [send(red_v.at[p, mine], red_v.at[p, mine], t) for t in in_plane]

    def sum_end(p, copies, count):
        for c in copies:
            c.wait_recv()
        total = added(p, zs, plane)
        return [
            jnp.concatenate([total[i * halves + h : i * halves + h + 1] for h in range(halves)], axis=1)
            for i in range(count)
        ]

    halo0 = []
    for h in range(halves):
        encode(0, h, s0_ref, most[:, h * LANES : (h + 1) * LANES])
        halo0.append(both_ways(0, h, halo0[h - 1] if h else ()))

    passed = []
    for side, copy in ((1, swapped[0]), (0, swapped[1])):
        copy.wait_recv()
        for other in others:
            passed.append(send(nbr_tiles.at[side, part], nbr_tiles.at[side, part], other))
    for c in passed:
        c.wait_recv()

    def theirs(r, _):
        w_v[0, r, :, LANES:] = nbr_tiles[0, inv_s[0, r]].T
        w_v[2, r, :, LANES:] = nbr_tiles[1, inv_s[2, r]].T
        return 0

    lax.fori_loop(0, rt, theirs, 0)

    for h in range(halves):
        apply_own(h, m0_ref)

    def first_use(carry, at, cut, m):
        most, curve = carry
        s0 = s0_ref[at, cut]
        return jnp.maximum(most, jnp.max(fold(m), axis=0)), curve + jnp.sum(fold(s0 * (s0 - DAMP * m)), axis=0)

    small = jnp.zeros((8, LANES), F32)
    halo1, curves = [], []
    for h in range(halves):
        decode(0, h, halo0[h])
        most, curve = apply(0, h, m0_ref, first_use, (small, small))
        curves.append(curve)
        last = h == halves - 1
        if last:
            on_way = sum_start(0, [square0, jnp.concatenate(curves, axis=1)])
        encode(1, h, m0_ref, most)
        if last:
            on_way = sum_middle(0, on_way)
        halo1.append(both_ways(1, h, halo1[h - 1] if h else halo0[-1]))
        apply_own(h, m1_ref)

    for h in range(halves - 1):
        decode(1, h, halo1[h])
        apply(1, h, m1_ref, lambda carry, at, cut, m: carry, 0)
    rr0, curve0 = sum_end(0, on_way, 2)
    alpha0 = rr0 / curve0

    def second_use(carry, at, cut, m1):
        s0, m0, a = s0_ref[at, cut], m0_ref[at, cut], alpha0[:, cut]
        s1 = s0 - DAMP * m0
        r1 = s0 - a * s1
        image = r1 - DAMP * (m0 - a * (m0 - DAMP * m1))
        return tuple(c + jnp.sum(fold(r1 * v), axis=0) for c, v in zip(carry, (r1, image, s1), strict=True))

    def second_pass(h):
        cut = slice(h * LANES, (h + 1) * LANES)

        def one(r, carry):
            at = pl.ds(pl.multiple_of(r * LANES, LANES), LANES)
            return second_use(carry, at, cut, m1_ref[at, cut])

        return lax.fori_loop(0, rt, one, (small, small, small))

    dots = [second_pass(h) for h in range(halves - 1)]
    decode(1, halves - 1, halo1[halves - 1])
    dots.append(apply(1, halves - 1, m1_ref, second_use, (small, small, small)))
    on_way = sum_start(1, [jnp.concatenate(d, axis=1) for d in zip(*dots, strict=True)])
    rr1, curve_rr, curve_rs = sum_end(1, sum_middle(1, on_way), 3)
    beta = rr1 / rr0
    curve1 = curve_rr + beta * (2.0 * curve_rs + beta * curve0)
    alpha1 = rr1 / curve1
    row = lax.broadcasted_iota(I32, (8, qdev), 0)
    coef_ref[...] = jnp.where(row == 0, alpha0, jnp.where(row == 1, beta, alpha1))

    for c in sent:
        c.wait_send()


def finish(s0_ref, m0_ref, m1_ref, coef_ref, rank_ref, resid_ref, rank_v, resid_v, sem):
    alpha0, beta, alpha1 = coef_ref[0:1], coef_ref[1:2], coef_ref[2:3]
    size = rank_ref.shape[0] // PIECES
    step = min(64, size)
    copies = []
    for p in range(PIECES):
        def one(i, _, p=p):
            at = pl.ds(pl.multiple_of(p * size + i * step, step), step)
            s0, m0 = s0_ref[at, :], m0_ref[at, :]
            r1 = s0 - alpha0 * (s0 - DAMP * m0)
            d1 = r1 + beta * s0
            image = d1 - DAMP * ((1.0 + beta) * m0 - alpha0 * (m0 - DAMP * m1_ref[at, :]))
            rank_v[at, :] = alpha0 * s0 + alpha1 * d1
            resid_v[at, :] = r1 - alpha1 * image
            return 0

        lax.fori_loop(0, size // step, one, 0)
        at = pl.ds(p * size, size)
        for i, (src, dst) in enumerate(((rank_v, rank_ref), (resid_v, resid_ref))):
            copies.append(pltpu.make_async_copy(src.at[at], dst.at[at], sem.at[i, p]))
            copies[-1].start()
    for c in copies:
        c.wait()


def body(descriptors, queries, tiles, tile_cols, part_size):
    n = lax.axis_size("vert")
    rows, width = descriptors.shape
    qdev, block = queries.shape
    rt = rows // LANES
    halves = qdev // LANES
    zs = n // (XS * YS)
    field = pltpu.VMEM((rows, qdev), F32)
    cores = lax.axis_size("qcol")
    copies = (2 * (zs - 1) + 2 * (XS + YS - 2)) + 2 * cores + 2 * halves * 4 + 2 * (XS * YS + zs - 2)
    s0, m0, m1, coef = pl.pallas_call(
        functools.partial(kernel, n),
        out_shape=(field, field, field, pltpu.VMEM((8, qdev), F32)),
        in_specs=[pl.BlockSpec(memory_space=pltpu.HBM)] * 5,
        out_specs=[pl.BlockSpec(memory_space=pltpu.VMEM)] * 4,
        scratch_shapes=[
            pltpu.VMEM((rows, width), BF16),
            pltpu.VMEM((3 * rt, LANES, LANES), BF16),
            pltpu.VMEM((2, rt, LANES, LANES), BF16),
            pltpu.VMEM((3, rt, LANES, 2 * LANES), BF16),
            pltpu.VMEM((halves, XS, YS, zs, block, LANES), BF16),
            pltpu.VMEM((width, qdev), BF16),
            pltpu.VMEM((2, halves, rt, LANES, LANES), jnp.int16),
            pltpu.VMEM((2, halves, 2, rt, LANES, LANES), jnp.int16),
            pltpu.VMEM((2, halves, 8, LANES), F32),
            pltpu.VMEM((2, halves, 2, 8, LANES), F32),
            pltpu.VMEM((halves, rt, LANES, 2 * LANES), BF16),
            pltpu.VMEM((2, rt, LANES, 2 * LANES), BF16),
            pltpu.VMEM((2, XS * YS + zs, 8, LANES), F32),
            pltpu.SMEM((3, rt, n), I32),
            pltpu.SMEM((n,), I32),
            pltpu.SMEM((3, rt), I32),
            pltpu.SemaphoreType.DMA((4 + halves,)),
            pltpu.SemaphoreType.DMA((copies,)),
            pltpu.SemaphoreType.DMA((copies,)),
        ],
        compiler_params=pltpu.CompilerParams(
            collective_id=0, has_side_effects=True, vmem_limit_bytes=40 * 2**20
        ),
    )(*(pltpu.with_memory_space_constraint(v, pltpu.HBM) for v in (descriptors, queries.T, tiles, jnp.transpose(tile_cols, (1, 2, 0)), part_size)))
    out = jax.ShapeDtypeStruct((rows, qdev), F32)
    return pl.pallas_call(
        finish,
        out_shape=(out, out),
        in_specs=[pl.BlockSpec(memory_space=pltpu.VMEM)] * 4,
        out_specs=[pl.BlockSpec(memory_space=pltpu.HBM)] * 2,
        scratch_shapes=[
            pltpu.VMEM((rows, qdev), F32),
            pltpu.VMEM((rows, qdev), F32),
            pltpu.SemaphoreType.DMA((2, PIECES)),
        ],
        compiler_params=pltpu.CompilerParams(vmem_limit_bytes=16 * 2**20),
    )(*(pltpu.with_memory_space_constraint(v, pltpu.VMEM) for v in (s0, m0, m1, coef)))


def solution(mesh):
    placed = (P("vert", None), P("qcol", "vert"), P("vert", None, None), P(), P())
    return jax.shard_map(
        body,
        mesh=mesh,
        in_specs=placed,
        out_specs=(P("vert", "qcol"), P("vert", "qcol")),
        check_vma=False,
    )
```

```python
import functools

import jax
import jax.numpy as jnp
from jax import lax
from jax.experimental import pallas as pl
from jax.experimental.pallas import tpu as pltpu
from jax.sharding import PartitionSpec as P

XS, YS = 4, 4
LANES = 128
STEPS = 65535.0
DAMP = 0.99
PIECES = 8
MESH = pl.DeviceIdType.MESH
F32, BF16, I32 = jnp.float32, jnp.bfloat16, jnp.int32


def kernel(
    n, desc_ref, q_ref, tiles_ref, cols_ref, size_ref,
    s0_ref, m0_ref, m1_ref, coef_ref,
    desc_v, tiles_v, nbr_tiles, w_v, qg, qcat, code_v, halo_v, scale_v, hscale_v, own_hl, halo_hl, red_v,
    cols_s, size_s, inv_s, local_sem, send_sem, recv_sem,
):
    zs = n // (XS * YS)
    rows = desc_ref.shape[0]
    rt = rows // LANES
    qdev = q_ref.shape[1]
    halves = qdev // LANES
    me = lax.axis_index("vert")
    x = lax.rem(me, XS)
    y = lax.rem(lax.div(me, XS), YS)
    z = lax.div(me, XS * YS)
    right, left = lax.rem(me + 1, n), lax.rem(me + n - 1, n)
    sizes = (XS, YS, zs)
    core, cores = lax.axis_index("qcol"), lax.axis_size("qcol")
    plane = XS * YS
    spot = lax.rem(me, plane)

    def peer(axis, k):
        if axis == 0:
            return me - x + lax.rem(x + k, XS)
        if axis == 1:
            return me + (lax.rem(y + k, YS) - y) * XS
        return lax.rem(me + k * (XS * YS), n)

    used = [0]
    sent = []

    def send(src, dst, target):
        i = used[0]
        used[0] += 1
        copy = pltpu.make_async_remote_copy(
            src_ref=src, dst_ref=dst, send_sem=send_sem.at[i], recv_sem=recv_sem.at[i],
            device_id=target if isinstance(target, dict) else {"vert": target}, device_id_type=MESH,
        )
        copy.start()
        sent.append(copy)
        return copy

    in_plane = [me - spot + lax.rem(y + j, YS) * XS + lax.rem(x + i, XS) for j in range(YS) for i in range(XS) if i or j]
    along_z = [peer(2, k) for k in range(1, zs)]
    others = [{"qcol": lax.rem(core + k, cores)} for k in range(1, cores)]
    partners = [{"vert": p} for p in in_plane + along_z + [right, left]] + others
    barrier = pltpu.get_barrier_semaphore()
    for p in partners:
        pl.semaphore_signal(barrier, inc=1, device_id=p, device_id_type=MESH)

    fetch_desc = pltpu.make_async_copy(desc_ref, desc_v, local_sem.at[0])
    fetch_desc.start()
    fetch_tiles = pltpu.make_async_copy(tiles_ref, tiles_v, local_sem.at[1])
    fetch_tiles.start()
    fetch_cols = pltpu.make_async_copy(cols_ref, cols_s, local_sem.at[2])
    fetch_cols.start()
    fetch_size = pltpu.make_async_copy(size_ref, size_s, local_sem.at[3])
    fetch_size.start()
    fetch_q = [
        pltpu.make_async_copy(q_ref.at[:, h * LANES : (h + 1) * LANES], qg.at[(h, *at, z)], local_sem.at[4 + h])
        for h, at in ((0, (x, y)), (1, (y, x)))
    ]
    for c in fetch_q:
        c.start()

    fetch_cols.wait()
    fetch_size.wait()
    live_count = size_s[me]
    parts = (left, me, right)
    for i in range(3):
        def invert(r, _, i=i):
            found = jnp.int32(0)
            for t in range(rt):
                found = jnp.where(cols_s[2 - i, t, parts[i]] == r, jnp.int32(t), found)
            inv_s[i, r] = found
            return 0

        lax.fori_loop(0, rt, invert, 0)

    fetch_tiles.wait()

    def ours(r, _):
        for i in range(3):
            w_v[i, r, :, :LANES] = tiles_v[i * rt + r]
        w_v[1, r, :, LANES:] = tiles_v[rt + inv_s[1, r]].T
        return 0

    lax.fori_loop(0, rt, ours, 0)

    for c in fetch_q:
        c.wait()
    pl.semaphore_wait(barrier, len(partners))

    step1 = [[send(qg.at[(h, *at, z)], qg.at[(h, *at, z)], t) for t in along_z] for h, at in ((0, (x, y)), (1, (y, x)))]
    for c in step1[0]:
        c.wait_recv()
    step2a = [send(qg.at[0, x, y], qg.at[0, x, y], peer(1, k)) for k in range(1, YS)]
    for c in step1[1]:
        c.wait_recv()
    step2b = [send(qg.at[1, y, x], qg.at[1, y, x], peer(0, k)) for k in range(1, XS)]
    for c in step2a:
        c.wait_recv()
    step3a = [send(qg.at[0, x], qg.at[0, x], peer(0, k)) for k in range(1, XS)]
    for c in step2b:
        c.wait_recv()
    step3b = [send(qg.at[1, y], qg.at[1, y], peer(1, k)) for k in range(1, YS)]

    def arrived(copies):
        for c in copies:
            c.wait_recv()

    def gathered(h):
        block = qg.shape[4]
        for zz in range(zs):
            for yy in range(YS):
                for xx in range(XS):
                    at = ((zz * YS + yy) * XS + xx) * block
                    qcat[h, at : at + block, :] = qg[(h, *((xx, yy) if h == 0 else (yy, xx)), zz)]

    arrived(step3a)
    share = rt // cores
    part = pl.ds(core * share, share)
    swapped = [
        send(tiles_v.at[pl.ds(core * share, share)], nbr_tiles.at[1, part], left),
        send(tiles_v.at[pl.ds(2 * rt + core * share, share)], nbr_tiles.at[0, part], right),
    ]
    gathered(0)

    fetch_desc.wait()

    chunk = min(1024, rows)

    def fold(values):
        return values.reshape(values.shape[0] // 8, 8, values.shape[1])

    def live_of(start, shape):
        return lax.broadcasted_iota(I32, shape, 0) + start < live_count

    small = jnp.zeros((8, LANES), F32)

    def seeds(h):
        cut = slice(h * LANES, (h + 1) * LANES)

        def one(i, carry):
            most, square = carry
            at = pl.ds(pl.multiple_of(i * chunk, chunk), chunk)
            sims = jnp.dot(desc_v[at, :], qcat[h], preferred_element_type=F32)
            pos = jnp.maximum(sims, 0.0)
            s = jnp.where(live_of(i * chunk, sims.shape), pos * pos * pos, 0.0)
            s0_ref[at, cut] = s
            return jnp.maximum(most, jnp.max(fold(s), axis=0)), square + jnp.sum(fold(s * s), axis=0)

        return lax.fori_loop(0, rows // chunk, one, (small, small))

    def encode(it, h, src_ref, most):
        cut = slice(h * LANES, (h + 1) * LANES)
        top = jnp.max(most, axis=0, keepdims=True)
        ok = top > 1e-30
        inverse = jnp.where(ok, STEPS / jnp.where(ok, top, 1.0), 0.0)
        scale_v[it, h] = jnp.broadcast_to(top * (1.0 / STEPS), (8, LANES))

        def one(r, _):
            at = pl.ds(pl.multiple_of(r * LANES, LANES), LANES)
            v = src_ref[at, cut]
            code_v[it, h, r] = ((v * inverse + 0.5).astype(I32) - 32768).astype(jnp.int16)
            hi = v.astype(BF16)
            own_hl[h, r, :, :LANES] = hi
            own_hl[h, r, :, LANES:] = (v - hi.astype(F32)).astype(BF16)
            return 0

        lax.fori_loop(0, rt, one, 0, unroll=4)

    def both_ways(it, h, after=()):
        for c in after:
            c.wait_send()
            sent[:] = [s for s in sent if s is not c]
        copies = []
        for side, target in ((1, left), (0, right)):
            copies.append(send(scale_v.at[it, h], hscale_v.at[it, h, side], target))
            copies.append(send(code_v.at[it, h], halo_v.at[it, h, side], target))
        return copies

    def decode(it, h, copies):
        for c in copies:
            c.wait_recv()
        for side in range(2):
            def one(r, _, side=side):
                v = halo_v[it, h, side, r].astype(I32) + 32768
                halo_hl[side, r, :, :LANES] = lax.shift_right_logical(v, 8).astype(F32).astype(BF16)
                halo_hl[side, r, :, LANES:] = lax.bitwise_and(v, 255).astype(F32).astype(BF16)
                return 0

            lax.fori_loop(0, rt, one, 0, unroll=4)

    def apply_own(h, out_ref):
        cut = slice(h * LANES, (h + 1) * LANES)

        def one(r, _):
            at = pl.ds(pl.multiple_of(r * LANES, LANES), LANES)
            from_own = jnp.dot(
                w_v[1, r],
                jnp.concatenate([own_hl[h, cols_s[1, r, me]], own_hl[h, inv_s[1, r]]], axis=0),
                preferred_element_type=F32,
            )
            out_ref[at, cut] = from_own[:, :LANES] + from_own[:, LANES:]
            return 0

        lax.fori_loop(0, rt, one, 0, unroll=4)

    def apply(it, h, out_ref, use, carry):
        cut = slice(h * LANES, (h + 1) * LANES)
        low, high = hscale_v[it, h, 0][:1], hscale_v[it, h, 1][:1]

        def one(r, carry):
            at = pl.ds(pl.multiple_of(r * LANES, LANES), LANES)
            from_left = jnp.dot(
                w_v[0, r],
                jnp.concatenate([halo_hl[0, cols_s[0, r, me]], halo_hl[0, inv_s[0, r]]], axis=0),
                preferred_element_type=F32,
            )
            from_right = jnp.dot(
                w_v[2, r],
                jnp.concatenate([halo_hl[1, cols_s[2, r, me]], halo_hl[1, inv_s[2, r]]], axis=0),
                preferred_element_type=F32,
            )
            total = (from_left[:, :LANES] * 256.0 + from_left[:, LANES:]) * low
            total = total + out_ref[at, cut]
            total = total + (from_right[:, :LANES] * 256.0 + from_right[:, LANES:]) * high
            m = jnp.where(live_of(r * LANES, total.shape), 0.5 * total, 0.0)
            out_ref[at, cut] = m
            return use(carry, at, cut, m)

        return lax.fori_loop(0, rt, one, carry, unroll=4)

    def sum_start(p, partials):
        row = lax.broadcasted_iota(I32, (8, LANES), 0)
        value = jnp.zeros((8, LANES), F32)
        for i, partial in enumerate(partials):
            for h in range(halves):
                sums = jnp.sum(partial[:, h * LANES : (h + 1) * LANES], axis=0, keepdims=True)
                value = jnp.where(row == i * halves + h, sums, value)
        red_v[p, z] = value
        return [send(red_v.at[p, z], red_v.at[p, z], t) for t in along_z]

    def added(p, first, count):
        value = red_v[p, first]
        for k in range(1, count):
            value = value + red_v[p, first + k]
        return value

    def sum_middle(p, copies):
        for c in copies:
            c.wait_recv()
        mine = zs + spot
        red_v[p, mine] = added(p, 0, zs)
        return [send(red_v.at[p, mine], red_v.at[p, mine], t) for t in in_plane]

    def sum_end(p, copies, count):
        for c in copies:
            c.wait_recv()
        total = added(p, zs, plane)
        return [
            jnp.concatenate([total[i * halves + h : i * halves + h + 1] for h in range(halves)], axis=1)
            for i in range(count)
        ]

    halo0, squares = [], []
    for h in range(halves):
        if h:
            arrived(step3b)
            gathered(1)
        most, square = seeds(h)
        squares.append(square)
        encode(0, h, s0_ref, most)
        halo0.append(both_ways(0, h))

    passed = []
    for side, copy in ((1, swapped[0]), (0, swapped[1])):
        copy.wait_recv()
        for other in others:
            passed.append(send(nbr_tiles.at[side, part], nbr_tiles.at[side, part], other))
    for c in passed:
        c.wait_recv()

    def theirs(r, _):
        w_v[0, r, :, LANES:] = nbr_tiles[0, inv_s[0, r]].T
        w_v[2, r, :, LANES:] = nbr_tiles[1, inv_s[2, r]].T
        return 0

    lax.fori_loop(0, rt, theirs, 0)

    for h in range(halves):
        apply_own(h, m0_ref)

    def first_use(carry, at, cut, m):
        most, curve = carry
        s0 = s0_ref[at, cut]
        return jnp.maximum(most, jnp.max(fold(m), axis=0)), curve + jnp.sum(fold(s0 * (s0 - DAMP * m)), axis=0)

    halo1, curves = [], []
    for h in range(halves):
        decode(0, h, halo0[h])
        most, curve = apply(0, h, m0_ref, first_use, (small, small))
        curves.append(curve)
        last = h == halves - 1
        if last:
            on_way = sum_start(0, [jnp.concatenate(v, axis=1) for v in (squares, curves)])
        encode(1, h, m0_ref, most)
        if last:
            on_way = sum_middle(0, on_way)
        halo1.append(both_ways(1, h))
        apply_own(h, m1_ref)

    for h in range(halves - 1):
        decode(1, h, halo1[h])
        apply(1, h, m1_ref, lambda carry, at, cut, m: carry, 0)
    rr0, curve0 = sum_end(0, on_way, 2)
    alpha0 = rr0 / curve0

    def second_use(carry, at, cut, m1):
        s0, m0, a = s0_ref[at, cut], m0_ref[at, cut], alpha0[:, cut]
        s1 = s0 - DAMP * m0
        r1 = s0 - a * s1
        image = r1 - DAMP * (m0 - a * (m0 - DAMP * m1))
        return tuple(c + jnp.sum(fold(r1 * v), axis=0) for c, v in zip(carry, (r1, image, s1), strict=True))

    def second_pass(h):
        cut = slice(h * LANES, (h + 1) * LANES)

        def one(r, carry):
            at = pl.ds(pl.multiple_of(r * LANES, LANES), LANES)
            return second_use(carry, at, cut, m1_ref[at, cut])

        return lax.fori_loop(0, rt, one, (small, small, small), unroll=4)

    dots = [second_pass(h) for h in range(halves - 1)]
    decode(1, halves - 1, halo1[halves - 1])
    dots.append(apply(1, halves - 1, m1_ref, second_use, (small, small, small)))
    on_way = sum_start(1, [jnp.concatenate(d, axis=1) for d in zip(*dots, strict=True)])
    rr1, curve_rr, curve_rs = sum_end(1, sum_middle(1, on_way), 3)
    beta = rr1 / rr0
    curve1 = curve_rr + beta * (2.0 * curve_rs + beta * curve0)
    alpha1 = rr1 / curve1
    row = lax.broadcasted_iota(I32, (8, qdev), 0)
    coef_ref[...] = jnp.where(row == 0, alpha0, jnp.where(row == 1, beta, alpha1))

    for c in sent:
        c.wait_send()


def finish(s0_ref, m0_ref, m1_ref, coef_ref, rank_ref, resid_ref, rank_v, resid_v, sem):
    alpha0, beta, alpha1 = coef_ref[0:1], coef_ref[1:2], coef_ref[2:3]
    size = rank_ref.shape[0] // PIECES
    step = min(64, size)
    copies = []
    for p in range(PIECES):
        def one(i, _, p=p):
            at = pl.ds(pl.multiple_of(p * size + i * step, step), step)
            s0, m0 = s0_ref[at, :], m0_ref[at, :]
            r1 = s0 - alpha0 * (s0 - DAMP * m0)
            d1 = r1 + beta * s0
            image = d1 - DAMP * ((1.0 + beta) * m0 - alpha0 * (m0 - DAMP * m1_ref[at, :]))
            rank_v[at, :] = alpha0 * s0 + alpha1 * d1
            resid_v[at, :] = r1 - alpha1 * image
            return 0

        lax.fori_loop(0, size // step, one, 0)
        at = pl.ds(p * size, size)
        for i, (src, dst) in enumerate(((rank_v, rank_ref), (resid_v, resid_ref))):
            copies.append(pltpu.make_async_copy(src.at[at], dst.at[at], sem.at[i, p]))
            copies[-1].start()
    for c in copies:
        c.wait()


def body(descriptors, queries, tiles, tile_cols, part_size):
    n = lax.axis_size("vert")
    rows, width = descriptors.shape
    qdev, block = queries.shape
    rt = rows // LANES
    halves = qdev // LANES
    zs = n // (XS * YS)
    field = pltpu.VMEM((rows, qdev), F32)
    cores = lax.axis_size("qcol")
    copies = (2 * (zs - 1) + 2 * (XS + YS - 2)) + 2 * cores + 2 * halves * 4 + 2 * (XS * YS + zs - 2)
    s0, m0, m1, coef = pl.pallas_call(
        functools.partial(kernel, n),
        out_shape=(field, field, field, pltpu.VMEM((8, qdev), F32)),
        in_specs=[pl.BlockSpec(memory_space=pltpu.HBM)] * 5,
        out_specs=[pl.BlockSpec(memory_space=pltpu.VMEM)] * 4,
        scratch_shapes=[
            pltpu.VMEM((rows, width), BF16),
            pltpu.VMEM((3 * rt, LANES, LANES), BF16),
            pltpu.VMEM((2, rt, LANES, LANES), BF16),
            pltpu.VMEM((3, rt, LANES, 2 * LANES), BF16),
            pltpu.VMEM((halves, XS, YS, zs, block, LANES), BF16),
            pltpu.VMEM((halves, width, LANES), BF16),
            pltpu.VMEM((2, halves, rt, LANES, LANES), jnp.int16),
            pltpu.VMEM((2, halves, 2, rt, LANES, LANES), jnp.int16),
            pltpu.VMEM((2, halves, 8, LANES), F32),
            pltpu.VMEM((2, halves, 2, 8, LANES), F32),
            pltpu.VMEM((halves, rt, LANES, 2 * LANES), BF16),
            pltpu.VMEM((2, rt, LANES, 2 * LANES), BF16),
            pltpu.VMEM((2, XS * YS + zs, 8, LANES), F32),
            pltpu.SMEM((3, rt, n), I32),
            pltpu.SMEM((n,), I32),
            pltpu.SMEM((3, rt), I32),
            pltpu.SemaphoreType.DMA((4 + halves,)),
            pltpu.SemaphoreType.DMA((copies,)),
            pltpu.SemaphoreType.DMA((copies,)),
        ],
        compiler_params=pltpu.CompilerParams(
            collective_id=0, has_side_effects=True, vmem_limit_bytes=40 * 2**20
        ),
    )(*(pltpu.with_memory_space_constraint(v, pltpu.HBM) for v in (descriptors, queries.T, tiles, jnp.transpose(tile_cols, (1, 2, 0)), part_size)))
    out = jax.ShapeDtypeStruct((rows, qdev), F32)
    return pl.pallas_call(
        finish,
        out_shape=(out, out),
        in_specs=[pl.BlockSpec(memory_space=pltpu.VMEM)] * 4,
        out_specs=[pl.BlockSpec(memory_space=pltpu.HBM)] * 2,
        scratch_shapes=[
            pltpu.VMEM((rows, qdev), F32),
            pltpu.VMEM((rows, qdev), F32),
            pltpu.SemaphoreType.DMA((2, PIECES)),
        ],
        compiler_params=pltpu.CompilerParams(vmem_limit_bytes=16 * 2**20),
    )(*(pltpu.with_memory_space_constraint(v, pltpu.VMEM) for v in (s0, m0, m1, coef)))


def solution(mesh):
    placed = (P("vert", None), P("qcol", "vert"), P("vert", None, None), P(), P())
    return jax.shard_map(
        body,
        mesh=mesh,
        in_specs=placed,
        out_specs=(P("vert", "qcol"), P("vert", "qcol")),
        check_vma=False,
    )
```

```python
import functools

import jax
import jax.numpy as jnp
from jax import lax
from jax.experimental import pallas as pl
from jax.experimental.pallas import tpu as pltpu
from jax.sharding import PartitionSpec as P

XS, YS = 4, 4
LANES = 128
STEPS = 65535.0
DAMP = 0.99
PIECES = 8
MESH = pl.DeviceIdType.MESH
F32, BF16, I32 = jnp.float32, jnp.bfloat16, jnp.int32


def kernel(
    n, desc_ref, q_ref, tiles_ref, cols_ref, size_ref,
    s0_ref, m0_ref, m1_ref, coef_ref,
    desc_v, tiles_v, nbr_tiles, w_v, qg, qcat, code_v, halo_v, scale_v, hscale_v, own_hl, halo_hl, red_v,
    cols_s, size_s, inv_s, local_sem, send_sem, recv_sem,
):
    zs = n // (XS * YS)
    rows = desc_ref.shape[0]
    rt = rows // LANES
    qdev = q_ref.shape[1]
    halves = qdev // LANES
    me = lax.axis_index("vert")
    x = lax.rem(me, XS)
    y = lax.rem(lax.div(me, XS), YS)
    z = lax.div(me, XS * YS)
    right, left = lax.rem(me + 1, n), lax.rem(me + n - 1, n)
    sizes = (XS, YS, zs)
    core, cores = lax.axis_index("qcol"), lax.axis_size("qcol")
    plane = XS * YS
    spot = lax.rem(me, plane)

    def peer(axis, k):
        if axis == 0:
            return me - x + lax.rem(x + k, XS)
        if axis == 1:
            return me + (lax.rem(y + k, YS) - y) * XS
        return lax.rem(me + k * (XS * YS), n)

    used = [0]
    sent = []

    def send(src, dst, target):
        i = used[0]
        used[0] += 1
        copy = pltpu.make_async_remote_copy(
            src_ref=src, dst_ref=dst, send_sem=send_sem.at[i], recv_sem=recv_sem.at[i],
            device_id=target if isinstance(target, dict) else {"vert": target}, device_id_type=MESH,
        )
        copy.start()
        sent.append(copy)
        return copy

    in_plane = [me - spot + lax.rem(y + j, YS) * XS + lax.rem(x + i, XS) for j in range(YS) for i in range(XS) if i or j]
    along_z = [peer(2, k) for k in range(1, zs)]
    others = [{"qcol": lax.rem(core + k, cores)} for k in range(1, cores)]
    partners = [{"vert": p} for p in in_plane + along_z + [right, left]] + others
    barrier = pltpu.get_barrier_semaphore()
    for p in partners:
        pl.semaphore_signal(barrier, inc=1, device_id=p, device_id_type=MESH)

    fetch_desc = pltpu.make_async_copy(desc_ref, desc_v, local_sem.at[0])
    fetch_desc.start()
    fetch_tiles = pltpu.make_async_copy(tiles_ref, tiles_v, local_sem.at[1])
    fetch_tiles.start()
    fetch_cols = pltpu.make_async_copy(cols_ref, cols_s, local_sem.at[2])
    fetch_cols.start()
    fetch_size = pltpu.make_async_copy(size_ref, size_s, local_sem.at[3])
    fetch_size.start()
    fetch_q = [
        pltpu.make_async_copy(q_ref.at[:, h * LANES : (h + 1) * LANES], qg.at[(h, *at, z)], local_sem.at[4 + h])
        for h, at in ((0, (x, y)), (1, (y, x)))
    ]
    for c in fetch_q:
        c.start()

    fetch_cols.wait()
    fetch_size.wait()
    live_count = size_s[me]
    parts = (left, me, right)
    for i in range(3):
        def invert(r, _, i=i):
            found = jnp.int32(0)
            for t in range(rt):
                found = jnp.where(cols_s[2 - i, t, parts[i]] == r, jnp.int32(t), found)
            inv_s[i, r] = found
            return 0

        lax.fori_loop(0, rt, invert, 0)

    fetch_tiles.wait()

    def ours(r, _):
        for i in range(3):
            w_v[i, r, :, :LANES] = tiles_v[i * rt + r]
        w_v[1, r, :, LANES:] = tiles_v[rt + inv_s[1, r]].T
        return 0

    lax.fori_loop(0, rt, ours, 0)

    for c in fetch_q:
        c.wait()
    pl.semaphore_wait(barrier, len(partners))

    step1 = [[send(qg.at[(h, *at, z)], qg.at[(h, *at, z)], t) for t in along_z] for h, at in ((0, (x, y)), (1, (y, x)))]
    for c in step1[0]:
        c.wait_recv()
    step2a = [send(qg.at[0, x, y], qg.at[0, x, y], peer(1, k)) for k in range(1, YS)]
    for c in step1[1]:
        c.wait_recv()
    step2b = [send(qg.at[1, y, x], qg.at[1, y, x], peer(0, k)) for k in range(1, XS)]
    for c in step2a:
        c.wait_recv()
    step3a = [send(qg.at[0, x], qg.at[0, x], peer(0, k)) for k in range(1, XS)]
    for c in step2b:
        c.wait_recv()
    step3b = [send(qg.at[1, y], qg.at[1, y], peer(1, k)) for k in range(1, YS)]

    def arrived(copies):
        for c in copies:
            c.wait_recv()

    def gathered(h):
        block = qg.shape[4]
        for zz in range(zs):
            for yy in range(YS):
                for xx in range(XS):
                    at = ((zz * YS + yy) * XS + xx) * block
                    qcat[h, at : at + block, :] = qg[(h, *((xx, yy) if h == 0 else (yy, xx)), zz)]

    arrived(step3a)
    share = rt // cores
    part = pl.ds(core * share, share)
    swapped = [
        send(tiles_v.at[pl.ds(core * share, share)], nbr_tiles.at[1, part], left),
        send(tiles_v.at[pl.ds(2 * rt + core * share, share)], nbr_tiles.at[0, part], right),
    ]
    gathered(0)

    fetch_desc.wait()

    chunk = min(1024, rows)

    def fold(values):
        return values.reshape(values.shape[0] // 8, 8, values.shape[1])

    def live_of(start, shape):
        return lax.broadcasted_iota(I32, shape, 0) + start < live_count

    small = jnp.zeros((8, LANES), F32)

    def seeds(h):
        cut = slice(h * LANES, (h + 1) * LANES)

        def one(i, carry):
            most, square = carry
            at = pl.ds(pl.multiple_of(i * chunk, chunk), chunk)
            sims = jnp.dot(desc_v[at, :], qcat[h], preferred_element_type=F32)
            pos = jnp.maximum(sims, 0.0)
            s = jnp.where(live_of(i * chunk, sims.shape), pos * pos * pos, 0.0)
            s0_ref[at, cut] = s
            return jnp.maximum(most, jnp.max(fold(s), axis=0)), square + jnp.sum(fold(s * s), axis=0)

        return lax.fori_loop(0, rows // chunk, one, (small, small))

    def encode(it, h, src_ref, most):
        cut = slice(h * LANES, (h + 1) * LANES)
        top = jnp.max(most, axis=0, keepdims=True)
        ok = top > 1e-30
        inverse = jnp.where(ok, STEPS / jnp.where(ok, top, 1.0), 0.0)
        scale_v[it, h] = jnp.broadcast_to(top * (1.0 / STEPS), (8, LANES))

        def one(r, _):
            at = pl.ds(pl.multiple_of(r * LANES, LANES), LANES)
            v = src_ref[at, cut]
            code_v[it, h, r] = ((v * inverse + 0.5).astype(I32) - 32768).astype(jnp.int16)
            hi = v.astype(BF16)
            own_hl[h, r, :, :LANES] = hi
            own_hl[h, r, :, LANES:] = (v - hi.astype(F32)).astype(BF16)
            return 0

        lax.fori_loop(0, rt, one, 0, unroll=4)

    def both_ways(it, h, after=()):
        for c in after:
            c.wait_send()
            sent[:] = [s for s in sent if s is not c]
        copies = []
        for side, target in ((1, left), (0, right)):
            copies.append(send(scale_v.at[it, h], hscale_v.at[it, h, side], target))
            copies.append(send(code_v.at[it, h], halo_v.at[it, h, side], target))
        return copies

    def decode(it, h, copies):
        for c in copies:
            c.wait_recv()
        for side in range(2):
            def one(r, _, side=side):
                v = halo_v[it, h, side, r].astype(I32) + 32768
                halo_hl[side, r, :, :LANES] = lax.shift_right_logical(v, 8).astype(F32).astype(BF16)
                halo_hl[side, r, :, LANES:] = lax.bitwise_and(v, 255).astype(F32).astype(BF16)
                return 0

            lax.fori_loop(0, rt, one, 0, unroll=4)

    def apply_own(h, out_ref):
        cut = slice(h * LANES, (h + 1) * LANES)

        def one(r, _):
            at = pl.ds(pl.multiple_of(r * LANES, LANES), LANES)
            from_own = jnp.dot(
                w_v[1, r],
                jnp.concatenate([own_hl[h, cols_s[1, r, me]], own_hl[h, inv_s[1, r]]], axis=0),
                preferred_element_type=F32,
            )
            out_ref[at, cut] = from_own[:, :LANES] + from_own[:, LANES:]
            return 0

        lax.fori_loop(0, rt, one, 0, unroll=4)

    def apply(it, h, out_ref, use, carry):
        cut = slice(h * LANES, (h + 1) * LANES)
        low, high = hscale_v[it, h, 0][:1], hscale_v[it, h, 1][:1]

        def one(r, carry):
            at = pl.ds(pl.multiple_of(r * LANES, LANES), LANES)
            from_left = jnp.dot(
                w_v[0, r],
                jnp.concatenate([halo_hl[0, cols_s[0, r, me]], halo_hl[0, inv_s[0, r]]], axis=0),
                preferred_element_type=F32,
            )
            from_right = jnp.dot(
                w_v[2, r],
                jnp.concatenate([halo_hl[1, cols_s[2, r, me]], halo_hl[1, inv_s[2, r]]], axis=0),
                preferred_element_type=F32,
            )
            total = (from_left[:, :LANES] * 256.0 + from_left[:, LANES:]) * low
            total = total + out_ref[at, cut]
            total = total + (from_right[:, :LANES] * 256.0 + from_right[:, LANES:]) * high
            m = jnp.where(live_of(r * LANES, total.shape), 0.5 * total, 0.0)
            out_ref[at, cut] = m
            return use(carry, at, cut, m)

        return lax.fori_loop(0, rt, one, carry, unroll=4)

    def sum_start(p, partials):
        row = lax.broadcasted_iota(I32, (8, LANES), 0)
        value = jnp.zeros((8, LANES), F32)
        for i, partial in enumerate(partials):
            for h in range(halves):
                sums = jnp.sum(partial[:, h * LANES : (h + 1) * LANES], axis=0, keepdims=True)
                value = jnp.where(row == i * halves + h, sums, value)
        red_v[p, z] = value
        return [send(red_v.at[p, z], red_v.at[p, z], t) for t in along_z]

    def added(p, first, count):
        value = red_v[p, first]
        for k in range(1, count):
            value = value + red_v[p, first + k]
        return value

    def sum_middle(p, copies):
        for c in copies:
            c.wait_recv()
        mine = zs + spot
        red_v[p, mine] = added(p, 0, zs)
        return [send(red_v.at[p, mine], red_v.at[p, mine], t) for t in in_plane]

    def sum_end(p, copies, count):
        for c in copies:
            c.wait_recv()
        total = added(p, zs, plane)
        return [
            jnp.concatenate([total[i * halves + h : i * halves + h + 1] for h in range(halves)], axis=1)
            for i in range(count)
        ]

    halo0, squares = [], []
    for h in range(halves):
        if h:
            arrived(step3b)
            gathered(1)
        most, square = seeds(h)
        squares.append(square)
        encode(0, h, s0_ref, most)
        halo0.append(both_ways(0, h))

    passed = []
    for side, copy in ((1, swapped[0]), (0, swapped[1])):
        copy.wait_recv()
        for other in others:
            passed.append(send(nbr_tiles.at[side, part], nbr_tiles.at[side, part], other))
    for c in passed:
        c.wait_recv()

    def theirs(r, _):
        w_v[0, r, :, LANES:] = nbr_tiles[0, inv_s[0, r]].T
        w_v[2, r, :, LANES:] = nbr_tiles[1, inv_s[2, r]].T
        return 0

    lax.fori_loop(0, rt, theirs, 0)

    for h in range(halves):
        apply_own(h, m0_ref)

    def first_use(carry, at, cut, m):
        most, curve = carry
        s0 = s0_ref[at, cut]
        return jnp.maximum(most, jnp.max(fold(m), axis=0)), curve + jnp.sum(fold(s0 * (s0 - DAMP * m)), axis=0)

    def drain(upto):
        for c in sent[:upto]:
            c.wait_send()
        del sent[:upto]

    before = len(sent)
    halo1, curves = [], []
    for h in range(halves):
        decode(0, h, halo0[h])
        most, curve = apply(0, h, m0_ref, first_use, (small, small))
        curves.append(curve)
        last = h == halves - 1
        if last:
            on_way = sum_start(0, [jnp.concatenate(v, axis=1) for v in (squares, curves)])
        encode(1, h, m0_ref, most)
        if last:
            on_way = sum_middle(0, on_way)
        halo1.append(both_ways(1, h))
        apply_own(h, m1_ref)

    for h in range(halves - 1):
        decode(1, h, halo1[h])
        apply(1, h, m1_ref, lambda carry, at, cut, m: carry, 0)
    rr0, curve0 = sum_end(0, on_way, 2)
    alpha0 = rr0 / curve0

    def second_use(carry, at, cut, m1):
        s0, m0, a = s0_ref[at, cut], m0_ref[at, cut], alpha0[:, cut]
        s1 = s0 - DAMP * m0
        r1 = s0 - a * s1
        image = r1 - DAMP * (m0 - a * (m0 - DAMP * m1))
        return tuple(c + jnp.sum(fold(r1 * v), axis=0) for c, v in zip(carry, (r1, image, s1), strict=True))

    def second_pass(h):
        cut = slice(h * LANES, (h + 1) * LANES)

        def one(r, carry):
            at = pl.ds(pl.multiple_of(r * LANES, LANES), LANES)
            return second_use(carry, at, cut, m1_ref[at, cut])

        return lax.fori_loop(0, rt, one, (small, small, small), unroll=4)

    drain(before)
    dots = [second_pass(h) for h in range(halves - 1)]
    decode(1, halves - 1, halo1[halves - 1])
    dots.append(apply(1, halves - 1, m1_ref, second_use, (small, small, small)))
    before = len(sent)
    on_way = sum_start(1, [jnp.concatenate(d, axis=1) for d in zip(*dots, strict=True)])
    drain(before)
    rr1, curve_rr, curve_rs = sum_end(1, sum_middle(1, on_way), 3)
    beta = rr1 / rr0
    curve1 = curve_rr + beta * (2.0 * curve_rs + beta * curve0)
    alpha1 = rr1 / curve1
    row = lax.broadcasted_iota(I32, (8, qdev), 0)
    coef_ref[...] = jnp.where(row == 0, alpha0, jnp.where(row == 1, beta, alpha1))

    drain(len(sent))


def finish(s0_ref, m0_ref, m1_ref, coef_ref, rank_ref, resid_ref, rank_v, resid_v, sem):
    alpha0, beta, alpha1 = coef_ref[0:1], coef_ref[1:2], coef_ref[2:3]
    size = rank_ref.shape[0] // PIECES
    step = min(64, size)
    copies = []
    for p in range(PIECES):
        def one(i, _, p=p):
            at = pl.ds(pl.multiple_of(p * size + i * step, step), step)
            s0, m0 = s0_ref[at, :], m0_ref[at, :]
            r1 = s0 - alpha0 * (s0 - DAMP * m0)
            d1 = r1 + beta * s0
            image = d1 - DAMP * ((1.0 + beta) * m0 - alpha0 * (m0 - DAMP * m1_ref[at, :]))
            rank_v[at, :] = alpha0 * s0 + alpha1 * d1
            resid_v[at, :] = r1 - alpha1 * image
            return 0

        lax.fori_loop(0, size // step, one, 0)
        at = pl.ds(p * size, size)
        for i, (src, dst) in enumerate(((rank_v, rank_ref), (resid_v, resid_ref))):
            copies.append(pltpu.make_async_copy(src.at[at], dst.at[at], sem.at[i, p]))
            copies[-1].start()
    for c in copies:
        c.wait()


def body(descriptors, queries, tiles, tile_cols, part_size):
    n = lax.axis_size("vert")
    rows, width = descriptors.shape
    qdev, block = queries.shape
    rt = rows // LANES
    halves = qdev // LANES
    zs = n // (XS * YS)
    field = pltpu.VMEM((rows, qdev), F32)
    cores = lax.axis_size("qcol")
    copies = (2 * (zs - 1) + 2 * (XS + YS - 2)) + 2 * cores + 2 * halves * 4 + 2 * (XS * YS + zs - 2)
    s0, m0, m1, coef = pl.pallas_call(
        functools.partial(kernel, n),
        out_shape=(field, field, field, pltpu.VMEM((8, qdev), F32)),
        in_specs=[pl.BlockSpec(memory_space=pltpu.HBM)] * 5,
        out_specs=[pl.BlockSpec(memory_space=pltpu.VMEM)] * 4,
        scratch_shapes=[
            pltpu.VMEM((rows, width), BF16),
            pltpu.VMEM((3 * rt, LANES, LANES), BF16),
            pltpu.VMEM((2, rt, LANES, LANES), BF16),
            pltpu.VMEM((3, rt, LANES, 2 * LANES), BF16),
            pltpu.VMEM((halves, XS, YS, zs, block, LANES), BF16),
            pltpu.VMEM((halves, width, LANES), BF16),
            pltpu.VMEM((2, halves, rt, LANES, LANES), jnp.int16),
            pltpu.VMEM((2, halves, 2, rt, LANES, LANES), jnp.int16),
            pltpu.VMEM((2, halves, 8, LANES), F32),
            pltpu.VMEM((2, halves, 2, 8, LANES), F32),
            pltpu.VMEM((halves, rt, LANES, 2 * LANES), BF16),
            pltpu.VMEM((2, rt, LANES, 2 * LANES), BF16),
            pltpu.VMEM((2, XS * YS + zs, 8, LANES), F32),
            pltpu.SMEM((3, rt, n), I32),
            pltpu.SMEM((n,), I32),
            pltpu.SMEM((3, rt), I32),
            pltpu.SemaphoreType.DMA((4 + halves,)),
            pltpu.SemaphoreType.DMA((copies,)),
            pltpu.SemaphoreType.DMA((copies,)),
        ],
        compiler_params=pltpu.CompilerParams(
            collective_id=0, has_side_effects=True, vmem_limit_bytes=40 * 2**20
        ),
    )(*(pltpu.with_memory_space_constraint(v, pltpu.HBM) for v in (descriptors, queries.T, tiles, jnp.transpose(tile_cols, (1, 2, 0)), part_size)))
    out = jax.ShapeDtypeStruct((rows, qdev), F32)
    return pl.pallas_call(
        finish,
        out_shape=(out, out),
        in_specs=[pl.BlockSpec(memory_space=pltpu.VMEM)] * 4,
        out_specs=[pl.BlockSpec(memory_space=pltpu.HBM)] * 2,
        scratch_shapes=[
            pltpu.VMEM((rows, qdev), F32),
            pltpu.VMEM((rows, qdev), F32),
            pltpu.SemaphoreType.DMA((2, PIECES)),
        ],
        compiler_params=pltpu.CompilerParams(vmem_limit_bytes=16 * 2**20),
    )(*(pltpu.with_memory_space_constraint(v, pltpu.VMEM) for v in (s0, m0, m1, coef)))


def solution(mesh):
    placed = (P("vert", None), P("qcol", "vert"), P("vert", None, None), P(), P())
    return jax.shard_map(
        body,
        mesh=mesh,
        in_specs=placed,
        out_specs=(P("vert", "qcol"), P("vert", "qcol")),
        check_vma=False,
    )
```
